512 devices in a mesh: section: 32 (over z, y_lo, core), tp: 4 (over y_hi), rep: 4 (over x).
Axes of the slice: x: 4, y: 8 (y_hi: 4, y_lo: 2; y = y_hi * 2 + y_lo), z: 8, core: 2. Of those that a mesh axis runs over, the one named last changes fastest.
Arguments:
- hidden: bfloat16 [32, 1536, 4096], P('section', 'rep', 'tp'), may hold values from -6 to 6
- cotangent: bfloat16 [32, 1536, 4096], P('section', 'rep', 'tp'), may hold values from -6 to 6
- w_down: bfloat16 [32, 4096, 1024], P('section', 'tp', 'rep'), may hold values from -0.09375 to 0.09375
- w_up: bfloat16 [32, 1024, 4096], P('section', 'rep', 'tp'), may hold values from -0.1875 to 0.1875
Outputs:
- rebuilt: bfloat16 [32, 1536, 4096], P('section', 'rep', 'tp')
- grad_hidden: bfloat16 [32, 1536, 4096], P('section', 'rep', 'tp')
- grad_up: bfloat16 [32, 1024, 4096], P('section', 'rep', 'tp')
- grad_down: bfloat16 [32, 4096, 1024], P('section', 'tp', 'rep')
The draws below stay inside these ranges and needn't reach their ends.
All inputs are finite; a program needn't handle non-finite values.
Results may differ from the reference program's by a relative error of at most 0.022.
Values may be sent and summed in bfloat16 or wider, within the bound.
No kernel may reach another device: no remote copies, remote signals or barrier semaphores. Data moves between devices by JAX's collectives and lax.ppermute only.
A program may use at most 64 MiB of HBM per device.

```python
import jax
import jax.numpy as jnp
from jax import lax

D = 4096
R = 1024
TOK_DEV = 384
SECTIONS = 32
TOKS = 1536
N_REP = 4


def levels(stream_key, shape, cuts, least, largest):
    def one(position, shards_of):
        heights = jax.random.uniform(jax.random.fold_in(jax.random.fold_in(stream_key, 6), position), (shards_of,), jnp.float32, least / len(cuts), largest / len(cuts))
        return jnp.repeat(jnp.exp(heights), shape[position] // shards_of).reshape((-1,) + (1,) * (len(shape) - position - 1))

    level = one(*cuts[0])
    for cut in cuts[1:]:
        level = level * one(*cut)
    return level


def bell_draw(key, extent, spread, most, shards=(), held_as=jnp.bfloat16):
    result = spread * jax.random.normal(key, extent, jnp.float32)
    if shards:
        result = result * levels(key, extent, shards, -0.22, 0.18)
    return jnp.clip(result, -most, most).astype(held_as)


def setup_inputs(seed: int = 0) -> dict:
    seeds = jax.random.split(jax.random.key(seed), 5)
    return {
        "hidden": bell_draw(seeds[0], (SECTIONS, TOKS, D), 1.0, 6.0, ((0, 32), (1, 4), (2, 4))),
        "cotangent": bell_draw(seeds[1], (SECTIONS, TOKS, D), 1.0, 6.0, ((0, 32), (1, 4), (2, 4))),
        "w_down": bell_draw(seeds[2], (SECTIONS, D, R), D ** -0.5, 0.09375, ((0, 32), (1, 4), (2, 4))),
        "w_up": bell_draw(seeds[3], (SECTIONS, R, D), R ** -0.5, 0.1875, ((0, 32), (1, 4), (2, 4))),
    }


def block_sum(left, right):
    total = jnp.zeros((left.shape[1], right.shape[1]), jnp.float32)
    for block in range(N_REP):
        lpart = left[block * TOK_DEV:(block + 1) * TOK_DEV]
        rpart = right[block * TOK_DEV:(block + 1) * TOK_DEV]
        term = jnp.dot(lpart.T, rpart, preferred_element_type=jnp.float32).astype(jnp.bfloat16)
        term = lax.optimization_barrier(term)
        total = total + term.astype(jnp.float32)
    return total.astype(jnp.bfloat16)


def reference(hidden, cotangent, w_down, w_up):
    code = lax.map(lambda pair: jnp.dot(pair[0], pair[1], preferred_element_type=jnp.float32).astype(jnp.bfloat16), (hidden, w_down))
    taken = jnp.roll(code, 1, axis=0)
    rebuilt = lax.map(lambda pair: jnp.dot(pair[0], pair[1], preferred_element_type=jnp.float32).astype(jnp.bfloat16), (taken, w_up))
    back = lax.map(lambda pair: jnp.dot(pair[0], pair[1].T, preferred_element_type=jnp.float32).astype(jnp.bfloat16), (cotangent, w_up))
    returned = jnp.roll(back, -1, axis=0)
    grad_hidden = lax.map(lambda pair: jnp.dot(pair[0], pair[1].T, preferred_element_type=jnp.float32).astype(jnp.bfloat16), (returned, w_down))
    grad_up = lax.map(lambda pair: block_sum(pair[0], pair[1]), (taken, cotangent))
    grad_down = lax.map(lambda pair: block_sum(pair[0], pair[1]), (hidden, returned))
    return rebuilt, grad_hidden, grad_up, grad_down
```

```python
import jax
import jax.numpy as jnp
from jax import lax
from jax.sharding import PartitionSpec as P

AXES = ("section", "tp", "rep")
EVEN = (1, 0, 3, 2)
ODD = (3, 2, 1, 0)


def route(sections, target):
    pairs = []
    for s in range(sections):
        for t in range(4):
            for r in range(4):
                a, b, c = target(s, t, r)
                pairs.append(((s * 4 + t) * 4 + r, ((a % sections) * 4 + b) * 4 + c))
    return pairs


def dot(left, right, dims):
    return lax.dot_general(left, right, (dims, ((), ())), preferred_element_type=jnp.float32)


def bf(x):
    return x.astype(jnp.bfloat16)


def f32(x):
    return x.astype(jnp.float32)


def shards(hidden, cotangent, w_down, w_up):
    sections = lax.axis_size("section")

    def send(x, target):
        return lax.ppermute(x, AXES, route(sections, target))

    def rep_pair(flip):
        table = (EVEN, ODD)
        return lambda s, t, r: (s, t, table[(s + flip) % 2][r])

    def tp_pair(flip, step=0):
        table = (EVEN, ODD)
        return lambda s, t, r: (s + step, table[(s + flip) % 2][t], r)

    parity = lax.axis_index("section") % 2
    tp = lax.axis_index("tp")
    v = ((tp == 1) | (tp == 2)).astype(jnp.int32)
    u = (tp >= 2).astype(jnp.int32)
    first = jnp.where(parity == 0, v, u)
    second = jnp.where(parity == 0, u, v)

    def reduce_and_shift(part, step):
        away = lax.dynamic_index_in_dim(part, 1 - first, 0, keepdims=False)
        came = send(away, tp_pair(0))
        kept = lax.dynamic_index_in_dim(part, first, 0, keepdims=False)
        half = bf(f32(kept) + f32(came))
        half = jnp.stack([half[:, :256], half[:, 256:]])
        over = lax.dynamic_index_in_dim(half, 1 - second, 0, keepdims=False)
        stay = lax.dynamic_index_in_dim(half, second, 0, keepdims=False)
        one = send(over, tp_pair(1, step))
        two = send(stay, lambda s, t, r: (s + step, t, r))
        return bf(f32(one) + f32(two))

    def gather(block):
        other = send(block, tp_pair(0))
        row = jnp.where(first == 0, jnp.concatenate([block, other], 1), jnp.concatenate([other, block], 1))
        rest = send(row, tp_pair(1))
        return jnp.where(second == 0, jnp.concatenate([row, rest], 0), jnp.concatenate([rest, row], 0))

    h, c, wd, wu = hidden[0], cotangent[0], w_down[0], w_up[0]
    h_in = send(h, rep_pair(0))
    wd_in = send(wd, rep_pair(1))
    c_in = send(c, rep_pair(1))
    wu_in = send(wu, rep_pair(0))
    hs = jnp.concatenate([h, h_in], 0)
    wds = jnp.concatenate([wd, wd_in], 1)
    cs = jnp.concatenate([c, c_in], 0)
    wus = jnp.concatenate([wu, wu_in], 0)
    code_part = bf(dot(hs, wds, ((1,), (0,)))).reshape(2, 384, 512)
    back_part = bf(dot(cs, wus, ((1,), (1,)))).reshape(2, 384, 512)
    code = gather(reduce_and_shift(code_part, 1))
    back = gather(reduce_and_shift(back_part, -1))
    r_out = bf(dot(code[384:], wus, ((1,), (0,))))
    r_in = send(r_out, rep_pair(1))
    u_out = bf(dot(code[:, 256:], cs, ((0,), (0,))))
    u_in = send(u_out, rep_pair(0))
    rebuilt = bf(dot(code[:384], wus, ((1,), (0,))) + f32(r_in))
    grad_up = bf(dot(code[:, :256], cs, ((0,), (0,))) + f32(u_in))
    g_out = bf(dot(back[384:], wds, ((1,), (1,))))
    g_in = send(g_out, rep_pair(0))
    d_out = bf(dot(hs, back[:, 256:], ((0,), (0,))))
    d_in = send(d_out, rep_pair(1))
    grad_hidden = bf(dot(back[:384], wds, ((1,), (1,))) + f32(g_in))
    grad_down = bf(dot(hs, back[:, :256], ((0,), (0,))) + f32(d_in))
    return (rebuilt[None], grad_hidden[None], grad_up[None], grad_down[None])


def solution(mesh):
    return jax.shard_map(
        shards,
        mesh=mesh,
        in_specs=(
            P("section", "rep", "tp"),
            P("section", "rep", "tp"),
            P("section", "tp", "rep"),
            P("section", "rep", "tp"),
        ),
        out_specs=(
            P("section", "rep", "tp"),
            P("section", "rep", "tp"),
            P("section", "rep", "tp"),
            P("section", "tp", "rep"),
        ),
        check_vma=False,
    )
```

```python
import jax
import jax.numpy as jnp
from jax import lax
from jax.sharding import PartitionSpec as P

AXES = ("section", "tp", "rep")
EVEN = (1, 0, 3, 2)
ODD = (3, 2, 1, 0)


def route(sections, target):
    pairs = []
    for s in range(sections):
        for t in range(4):
            for r in range(4):
                a, b, c = target(s, t, r)
                pairs.append(((s * 4 + t) * 4 + r, ((a % sections) * 4 + b) * 4 + c))
    return pairs


def dot(left, right, dims):
    return lax.dot_general(left, right, (dims, ((), ())), preferred_element_type=jnp.float32)


def bf(x):
    return x.astype(jnp.bfloat16)


def f32(x):
    return x.astype(jnp.float32)


barrier = lax.optimization_barrier


def shards(hidden, cotangent, w_down, w_up):
    sections = lax.axis_size("section")

    def send(x, target):
        return lax.ppermute(x, AXES, route(sections, target))

    def rep_pair(flip):
        table = (EVEN, ODD)
        return lambda s, t, r: (s, t, table[(s + flip) % 2][r])

    def tp_pair(flip, step=0):
        table = (EVEN, ODD)
        return lambda s, t, r: (s + step, table[(s + flip) % 2][t], r)

    parity = lax.axis_index("section") % 2
    tp = lax.axis_index("tp")
    v = ((tp == 1) | (tp == 2)).astype(jnp.int32)
    u = (tp >= 2).astype(jnp.int32)
    first = jnp.where(parity == 0, v, u)
    second = jnp.where(parity == 0, u, v)

    def pick(bit, zero, one):
        return jnp.where(bit == 0, zero, one)

    def reduce_and_shift(own, other, weight, dims, step):
        away = bf(dot(pick(first, other, own), weight, dims))
        came = send(away, tp_pair(0))
        kept = bf(dot(pick(first, own, other), weight, dims))
        half = bf(f32(kept) + f32(came))
        one = send(half, tp_pair(1, step))
        two = send(half, lambda s, t, r: (s + step, t, r))
        return bf(f32(one) + f32(two))

    def complete(half):
        rest = send(half, tp_pair(1))
        return pick(second, half, rest), pick(second, rest, half)

    h, c, wd, wu = hidden[0], cotangent[0], w_down[0], w_up[0]
    c_in = send(c, rep_pair(1))
    wu_in = send(wu, rep_pair(0))
    h_in = send(h, rep_pair(0))
    wd_in = send(wd, rep_pair(1))
    wus = jnp.concatenate([wu, wu_in], 0)
    back_half = reduce_and_shift(c, c_in, wus, ((1,), (1,)), -1)
    wds = jnp.concatenate([wd, wd_in], 1)
    code_half = reduce_and_shift(h, h_in, wds, ((1,), (0,)), 1)
    hs = jnp.concatenate([h, h_in], 0)
    cs = jnp.concatenate([c, c_in], 0)
    back_own, back_other = complete(back_half)
    back = jnp.concatenate([back_own, back_other], 0)
    g_out = bf(dot(back_other, wds, ((1,), (1,))))
    d_out = bf(dot(hs, back[:, 256:], ((0,), (0,))))
    code_half, g_out, d_out = barrier((code_half, g_out, d_out))
    g_in = send(g_out, rep_pair(0))
    d_in = send(d_out, rep_pair(1))
    g_own = dot(back_own, wds, ((1,), (1,)))
    d_own = dot(hs, back[:, :256], ((0,), (0,)))
    code_own, code_other = complete(code_half)
    code = jnp.concatenate([code_own, code_other], 0)
    r_out = bf(dot(code_other, wus, ((1,), (0,))))
    r_in = send(r_out, rep_pair(1))
    u_out = bf(dot(code[:, 256:], cs, ((0,), (0,))))
    u_in = send(u_out, rep_pair(0))
    r_own = dot(code_own, wus, ((1,), (0,)))
    u_own = dot(code[:, :256], cs, ((0,), (0,)))
    r_own, u_own, g_own, d_own = barrier((r_own, u_own, g_own, d_own))
    grad_hidden = bf(g_own + f32(g_in))
    grad_down = bf(d_own + f32(d_in))
    rebuilt = bf(r_own + f32(r_in))
    grad_up = bf(u_own + f32(u_in))
    return (rebuilt[None], grad_hidden[None], grad_up[None], grad_down[None])


def solution(mesh):
    return jax.shard_map(
        shards,
        mesh=mesh,
        in_specs=(
            P("section", "rep", "tp"),
            P("section", "rep", "tp"),
            P("section", "tp", "rep"),
            P("section", "rep", "tp"),
        ),
        out_specs=(
            P("section", "rep", "tp"),
            P("section", "rep", "tp"),
            P("section", "rep", "tp"),
            P("section", "tp", "rep"),
        ),
        check_vma=False,
    )
```

```python
import jax
import jax.numpy as jnp
from jax import lax
from jax.sharding import PartitionSpec as P

AXES = ("section", "tp", "rep")
EVEN = (1, 0, 3, 2)
ODD = (3, 2, 1, 0)


def route(sections, target):
    pairs = []
    for s in range(sections):
        for t in range(4):
            for r in range(4):
                a, b, c = target(s, t, r)
                pairs.append(((s * 4 + t) * 4 + r, ((a % sections) * 4 + b) * 4 + c))
    return pairs


def dot(left, right, dims):
    return lax.dot_general(left, right, (dims, ((), ())), preferred_element_type=jnp.float32)


def bf(x):
    return x.astype(jnp.bfloat16)


def f32(x):
    return x.astype(jnp.float32)


barrier = lax.optimization_barrier


def shards(hidden, cotangent, w_down, w_up):
    sections = lax.axis_size("section")

    def send(x, target):
        return lax.ppermute(x, AXES, route(sections, target))

    def rep_pair(flip):
        table = (EVEN, ODD)
        return lambda s, t, r: (s, t, table[(s + flip) % 2][r])

    def tp_pair(flip, step=0):
        table = (EVEN, ODD)
        return lambda s, t, r: (s + step, table[(s + flip) % 2][t], r)

    parity = lax.axis_index("section") % 2
    tp = lax.axis_index("tp")
    v = ((tp == 1) | (tp == 2)).astype(jnp.int32)
    u = (tp >= 2).astype(jnp.int32)
    first = jnp.where(parity == 0, v, u)
    second = jnp.where(parity == 0, u, v)

    def pick(bit, zero, one):
        return jnp.where(bit == 0, zero, one)

    def half_sum(own, other, weight, dims):
        away = bf(dot(pick(first, other, own), weight, dims))
        came = send(away, tp_pair(0))
        kept = bf(dot(pick(first, own, other), weight, dims))
        return bf(f32(kept) + f32(came))

    def shift(half, step):
        one = send(half, tp_pair(1, step))
        two = send(half, lambda s, t, r: (s + step, t, r))
        return one, two

    def gather_pairs(half):
        groups = []
        for at in range(sections):
            for one, two in ((0, 1), (3, 2)) if at % 2 == 1 else ((0, 3), (1, 2)):
                for r in range(4):
                    groups.append([(at * 4 + one) * 4 + r, (at * 4 + two) * 4 + r])
        both = lax.all_gather(half, AXES, axis=0, tiled=True, axis_index_groups=groups)
        return both[:384], both[384:]

    def other_half(half):
        return send(half, tp_pair(1))

    def in_order(half, rest):
        return pick(second, half, rest), pick(second, rest, half)

    h, c, wd, wu = hidden[0], cotangent[0], w_down[0], w_up[0]
    c_in = send(c, rep_pair(1))
    wu_in = send(wu, rep_pair(0))
    h_in = send(h, rep_pair(0))
    wd_in = send(wd, rep_pair(1))
    back_half = half_sum(c, c_in, jnp.concatenate([wu, wu_in], 0), ((1,), (1,)))
    code_half = half_sum(h, h_in, jnp.concatenate([wd, wd_in], 1), ((1,), (0,)))
    back_half, back_kept = shift(back_half, -1)
    code_half, code_kept = shift(code_half, 1)
    back_kept, wu, wd, wu_in, wd_in = barrier((back_kept, wu, wd, wu_in, wd_in))
    wus = barrier(jnp.concatenate([wu, wu_in], 0))
    wds = barrier(jnp.concatenate([wd, wd_in], 1))
    back_half = bf(f32(back_half) + f32(back_kept))
    code_half = bf(f32(code_half) + f32(code_kept))
    wus_far = send(wus, rep_pair(1))
    wds_far = send(wds, rep_pair(0))
    code_half, wus_far, wds_far = barrier((code_half, wus_far, wds_far))
    hs = barrier(jnp.concatenate([h, h_in], 0))
    cs = barrier(jnp.concatenate([c, c_in], 0))
    back_own, back_other = gather_pairs(back_half)
    code_rest = other_half(code_half)
    back_far = send(back_other, rep_pair(0))
    back = jnp.concatenate([back_own, back_other], 0)
    d_out = bf(dot(hs, back[:, 256:], ((0,), (0,))))
    d_in = send(d_out, rep_pair(1))
    g_own = dot(back_own, wds, ((1,), (1,)))
    d_own = dot(hs, back[:, :256], ((0,), (0,)))
    code_rest, d_out, g_own, d_own = barrier((code_rest, d_out, g_own, d_own))
    code_own, code_other = in_order(code_half, code_rest)
    code_far = send(code_other, rep_pair(1))
    code = jnp.concatenate([code_own, code_other], 0)
    u_out = bf(dot(code[:, 256:], cs, ((0,), (0,))))
    u_in = send(u_out, rep_pair(0))
    code_own, code, u_out = barrier((code_own, code, u_out))
    r_own = dot(code_own, wus, ((1,), (0,)))
    u_own = dot(code[:, :256], cs, ((0,), (0,)))
    r_own, u_own = barrier((r_own, u_own))
    grad_hidden = bf(g_own + dot(back_far, wds_far, ((1,), (1,))))
    grad_down = bf(d_own + f32(d_in))
    rebuilt = bf(r_own + dot(code_far, wus_far, ((1,), (0,))))
    grad_up = bf(u_own + f32(u_in))
    return (rebuilt[None], grad_hidden[None], grad_up[None], grad_down[None])


def solution(mesh):
    return jax.shard_map(
        shards,
        mesh=mesh,
        in_specs=(
            P("section", "rep", "tp"),
            P("section", "rep", "tp"),
            P("section", "tp", "rep"),
            P("section", "rep", "tp"),
        ),
        out_specs=(
            P("section", "rep", "tp"),
            P("section", "rep", "tp"),
            P("section", "rep", "tp"),
            P("section", "tp", "rep"),
        ),
        check_vma=False,
    )
```

```python
import jax
import jax.numpy as jnp
from jax import lax
from jax.sharding import PartitionSpec as P

AXES = ("section", "tp", "rep")
EVEN = (1, 0, 3, 2)
ODD = (3, 2, 1, 0)


def route(sections, target):
    pairs = []
    for s in range(sections):
        for t in range(4):
            for r in range(4):
                a, b, c = target(s, t, r)
                pairs.append(((s * 4 + t) * 4 + r, ((a % sections) * 4 + b) * 4 + c))
    return pairs


def dot(left, right, dims):
    return lax.dot_general(left, right, (dims, ((), ())), preferred_element_type=jnp.float32)


def bf(x):
    return x.astype(jnp.bfloat16)


def f32(x):
    return x.astype(jnp.float32)


barrier = lax.optimization_barrier


def shards(hidden, cotangent, w_down, w_up):
    sections = lax.axis_size("section")

    def send(x, target):
        return lax.ppermute(x, AXES, route(sections, target))

    def rep_pair(flip):
        table = (EVEN, ODD)
        return lambda s, t, r: (s, t, table[(s + flip) % 2][r])

    def tp_pair(flip, step=0):
        table = (EVEN, ODD)
        return lambda s, t, r: (s + step, table[(s + flip) % 2][t], r)

    parity = lax.axis_index("section") % 2
    tp = lax.axis_index("tp")
    v = ((tp == 1) | (tp == 2)).astype(jnp.int32)
    u = (tp >= 2).astype(jnp.int32)
    first = jnp.where(parity == 0, v, u)
    second = jnp.where(parity == 0, u, v)

    def pick(bit, zero, one):
        return jnp.where(bit == 0, zero, one)

    def half_sum(own, other, weight, dims):
        away = bf(dot(pick(first, other, own), weight, dims))
        came = send(away, tp_pair(0))
        kept = bf(dot(pick(first, own, other), weight, dims))
        return bf(f32(kept) + f32(came))

    def shift(half, step):
        one = send(half, tp_pair(1, step))
        two = send(half, lambda s, t, r: (s + step, t, r))
        return one, two

    def other_half(half):
        return send(half, tp_pair(1))

    def in_order(half, rest):
        return pick(second, half, rest), pick(second, rest, half)

    h, c, wd, wu = hidden[0], cotangent[0], w_down[0], w_up[0]
    c_in = send(c, rep_pair(1))
    wu_in = send(wu, rep_pair(0))
    h_in = send(h, rep_pair(0))
    wd_in = send(wd, rep_pair(1))
    back_half = half_sum(c, c_in, jnp.concatenate([wu, wu_in], 0), ((1,), (1,)))
    code_half = half_sum(h, h_in, jnp.concatenate([wd, wd_in], 1), ((1,), (0,)))
    back_half, back_kept = shift(back_half, -1)
    code_half, wu, wd, wu_in, wd_in = barrier((code_half, wu, wd, wu_in, wd_in))
    code_half, code_kept = shift(code_half, 1)
    wus = barrier(jnp.concatenate([wu, wu_in], 0))
    wds = barrier(jnp.concatenate([wd, wd_in], 1))
    back_half = bf(f32(back_half) + f32(back_kept))
    code_half = bf(f32(code_half) + f32(code_kept))
    wus_far = send(wus, rep_pair(1))
    wds_far = send(wds, rep_pair(0))
    hs = barrier(jnp.concatenate([h, h_in], 0))
    cs = barrier(jnp.concatenate([c, c_in], 0))
    back_own, back_other = in_order(back_half, other_half(back_half))
    code_rest = other_half(code_half)
    back = jnp.concatenate([back_own, back_other], 0)
    back_far = send(back_other, rep_pair(0))
    d_out = bf(dot(hs, back[:, 256:], ((0,), (0,))))
    d_in = send(d_out, rep_pair(1))
    g_own = dot(back_own, wds, ((1,), (1,)))
    d_own = dot(hs, back[:, :256], ((0,), (0,)))
    code_rest, d_out, wus_far, wds_far = barrier((code_rest, d_out, wus_far, wds_far))
    code_own, code_other = in_order(code_half, code_rest)
    code_far = send(code_other, rep_pair(1))
    code = jnp.concatenate([code_own, code_other], 0)
    u_out = bf(dot(code[:, 256:], cs, ((0,), (0,))))
    u_in = send(u_out, rep_pair(0))
    code_own, code, u_out, back_far = barrier((code_own, code, u_out, back_far))
    r_own = dot(code_own, wus, ((1,), (0,)))
    u_own = dot(code[:, :256], cs, ((0,), (0,)))
    r_own, u_own = barrier((r_own, u_own))
    grad_hidden = bf(g_own + dot(back_far, wds_far, ((1,), (1,))))
    grad_down = bf(d_own + f32(d_in))
    rebuilt = bf(r_own + dot(code_far, wus_far, ((1,), (0,))))
    grad_hidden, grad_down, rebuilt, u_in = barrier((grad_hidden, grad_down, rebuilt, u_in))
    grad_up = bf(u_own + f32(u_in))
    return (rebuilt[None], grad_hidden[None], grad_up[None], grad_down[None])


def solution(mesh):
    return jax.shard_map(
        shards,
        mesh=mesh,
        in_specs=(
            P("section", "rep", "tp"),
            P("section", "rep", "tp"),
            P("section", "tp", "rep"),
            P("section", "rep", "tp"),
        ),
        out_specs=(
            P("section", "rep", "tp"),
            P("section", "rep", "tp"),
            P("section", "rep", "tp"),
            P("section", "tp", "rep"),
        ),
        check_vma=False,
    )
```

```python
import jax
import jax.numpy as jnp
from jax import lax
from jax.sharding import PartitionSpec as P

AXES = ("section", "tp", "rep")
EVEN = (1, 0, 3, 2)
ODD = (3, 2, 1, 0)


def route(sections, target):
    pairs = []
    for s in range(sections):
        for t in range(4):
            for r in range(4):
                a, b, c = target(s, t, r)
                pairs.append(((s * 4 + t) * 4 + r, ((a % sections) * 4 + b) * 4 + c))
    return pairs


def dot(left, right, dims):
    return lax.dot_general(left, right, (dims, ((), ())), preferred_element_type=jnp.float32)


def bf(x):
    return x.astype(jnp.bfloat16)


def f32(x):
    return x.astype(jnp.float32)


barrier = lax.optimization_barrier


def shards(hidden, cotangent, w_down, w_up):
    sections = lax.axis_size("section")

    def send(x, target):
        return lax.ppermute(x, AXES, route(sections, target))

    def rep_pair(flip):
        table = (EVEN, ODD)
        return lambda s, t, r: (s, t, table[(s + flip) % 2][r])

    def tp_pair(flip, step=0):
        table = (EVEN, ODD)
        return lambda s, t, r: (s + step, table[(s + flip) % 2][t], r)

    parity = lax.axis_index("section") % 2
    tp = lax.axis_index("tp")
    v = ((tp == 1) | (tp == 2)).astype(jnp.int32)
    u = (tp >= 2).astype(jnp.int32)
    first = jnp.where(parity == 0, v, u)
    second = jnp.where(parity == 0, u, v)

    def pick(bit, zero, one):
        return jnp.where(bit == 0, zero, one)

    def half_sum(own, other, weight, dims):
        away = bf(dot(pick(first, other, own), weight, dims))
        came = send(away, tp_pair(0))
        kept = bf(dot(pick(first, own, other), weight, dims))
        return bf(f32(kept) + f32(came))

    def shift(half, step):
        two = send(half, lambda s, t, r: (s + step, t, r))
        one = send(half, tp_pair(1, step))
        return two, one

    def other_half(half):
        return send(half, tp_pair(1))

    def in_order(half, rest):
        return pick(second, half, rest), pick(second, rest, half)

    h, c, wd, wu = hidden[0], cotangent[0], w_down[0], w_up[0]
    c_in = send(c, rep_pair(1))
    wu_in = send(wu, rep_pair(0))
    h_in = send(h, rep_pair(0))
    wd_in = send(wd, rep_pair(1))
    back_half = half_sum(c, c_in, jnp.concatenate([wu, wu_in], 0), ((1,), (1,)))
    code_half = half_sum(h, h_in, jnp.concatenate([wd, wd_in], 1), ((1,), (0,)))
    back_half, back_kept = shift(back_half, -1)
    code_half, wu, wd, wu_in, wd_in = barrier((code_half, wu, wd, wu_in, wd_in))
    code_half, code_kept = shift(code_half, 1)
    wus = barrier(jnp.concatenate([wu, wu_in], 0))
    wds = barrier(jnp.concatenate([wd, wd_in], 1))
    back_half = bf(f32(back_half) + f32(back_kept))
    code_half = bf(f32(code_half) + f32(code_kept))
    wus_far = send(wus, rep_pair(1))
    wds_far = send(wds, rep_pair(0))
    hs = barrier(jnp.concatenate([h, h_in], 0))
    cs = barrier(jnp.concatenate([c, c_in], 0))
    back_own, back_other = in_order(back_half, other_half(back_half))
    code_rest = other_half(code_half)
    back = jnp.concatenate([back_own, back_other], 0)
    back_far = send(back_other, rep_pair(0))
    d_out = bf(dot(hs, back[:, 256:], ((0,), (0,))))
    d_in = send(d_out, rep_pair(1))
    g_own = dot(back_own, wds, ((1,), (1,)))
    d_own = dot(hs, back[:, :256], ((0,), (0,)))
    code_rest, d_out, wus_far, wds_far = barrier((code_rest, d_out, wus_far, wds_far))
    code_own, code_other = in_order(code_half, code_rest)
    code = jnp.concatenate([code_own, code_other], 0)
    u_out = bf(dot(code[:, 256:], cs, ((0,), (0,))))
    u_in = send(u_out, rep_pair(0))
    u_out, code_other = barrier((u_out, code_other))
    code_far = send(code_other, rep_pair(1))
    code_own, code, u_out, back_far = barrier((code_own, code, u_out, back_far))
    r_own = dot(code_own, wus, ((1,), (0,)))
    u_own = dot(code[:, :256], cs, ((0,), (0,)))
    r_own, u_own = barrier((r_own, u_own))
    grad_hidden = bf(g_own + dot(back_far, wds_far, ((1,), (1,))))
    grad_down = bf(d_own + f32(d_in))
    rebuilt = bf(r_own + dot(code_far, wus_far, ((1,), (0,))))
    grad_hidden, grad_down, rebuilt, u_in = barrier((grad_hidden, grad_down, rebuilt, u_in))
    grad_up = bf(u_own + f32(u_in))
    return (rebuilt[None], grad_hidden[None], grad_up[None], grad_down[None])


def solution(mesh):
    return jax.shard_map(
        shards,
        mesh=mesh,
        in_specs=(
            P("section", "rep", "tp"),
            P("section", "rep", "tp"),
            P("section", "tp", "rep"),
            P("section", "rep", "tp"),
        ),
        out_specs=(
            P("section", "rep", "tp"),
            P("section", "rep", "tp"),
            P("section", "rep", "tp"),
            P("section", "tp", "rep"),
        ),
        check_vma=False,
    )
```

```python
import jax
import jax.numpy as jnp
from jax import lax
from jax.sharding import PartitionSpec as P

AXES = ("section", "tp", "rep")
EVEN = (1, 0, 3, 2)
ODD = (3, 2, 1, 0)


def route(sections, target):
    pairs = []
    for s in range(sections):
        for t in range(4):
            for r in range(4):
                a, b, c = target(s, t, r)
                pairs.append(((s * 4 + t) * 4 + r, ((a % sections) * 4 + b) * 4 + c))
    return pairs


def dot(left, right, dims):
    return lax.dot_general(left, right, (dims, ((), ())), preferred_element_type=jnp.float32)


def bf(x):
    return x.astype(jnp.bfloat16)


def f32(x):
    return x.astype(jnp.float32)


barrier = lax.optimization_barrier


def shards(hidden, cotangent, w_down, w_up):
    sections = lax.axis_size("section")

    def send(x, target):
        return lax.ppermute(x, AXES, route(sections, target))

    def rep_pair(flip):
        table = (EVEN, ODD)
        return lambda s, t, r: (s, t, table[(s + flip) % 2][r])

    def tp_pair(flip, step=0):
        table = (EVEN, ODD)
        return lambda s, t, r: (s + step, table[(s + flip) % 2][t], r)

    parity = lax.axis_index("section") % 2
    tp = lax.axis_index("tp")
    v = ((tp == 1) | (tp == 2)).astype(jnp.int32)
    u = (tp >= 2).astype(jnp.int32)
    first = jnp.where(parity == 0, v, u)
    second = jnp.where(parity == 0, u, v)

    def pick(bit, zero, one):
        return jnp.where(bit == 0, zero, one)

    def half_sum(own, other, weight, dims):
        away = bf(dot(pick(first, other, own), weight, dims))
        came = send(away, tp_pair(0))
        kept = bf(dot(pick(first, own, other), weight, dims))
        return bf(f32(kept) + f32(came))

    def shift(half, step):
        two = send(half, lambda s, t, r: (s + step, t, r))
        one = send(half, tp_pair(1, step))
        return two, one

    def other_half(half):
        return send(half, tp_pair(1))

    def in_order(half, rest):
        return pick(second, half, rest), pick(second, rest, half)

    h, c, wd, wu = hidden[0], cotangent[0], w_down[0], w_up[0]
    c_in = send(c, rep_pair(1))
    wu_in = send(wu, rep_pair(0))
    h_in = send(h, rep_pair(0))
    wd_in = send(wd, rep_pair(1))
    back_half = half_sum(c, c_in, jnp.concatenate([wu, wu_in], 0), ((1,), (1,)))
    code_half = half_sum(h, h_in, jnp.concatenate([wd, wd_in], 1), ((1,), (0,)))
    back_half, back_kept = shift(back_half, -1)
    code_half, wu, wd, wu_in, wd_in = barrier((code_half, wu, wd, wu_in, wd_in))
    code_half, code_kept = shift(code_half, 1)
    wus = barrier(jnp.concatenate([wu, wu_in], 0))
    wds = barrier(jnp.concatenate([wd, wd_in], 1))
    back_half = bf(f32(back_half) + f32(back_kept))
    code_half = bf(f32(code_half) + f32(code_kept))
    wus_far = send(wus, rep_pair(1))
    wds_far = send(wds, rep_pair(0))
    hs = barrier(jnp.concatenate([h, h_in], 0))
    cs = barrier(jnp.concatenate([c, c_in], 0))
    back_own, back_other = in_order(back_half, other_half(back_half))
    code_rest = other_half(code_half)
    back = jnp.concatenate([back_own, back_other], 0)
    d_out = bf(dot(hs, back[:, 256:], ((0,), (0,))))
    d_in = send(d_out, rep_pair(1))
    d_out, back_other = barrier((d_out, back_other))
    back_far = send(back_other, rep_pair(0))
    g_own = dot(back_own, wds, ((1,), (1,)))
    d_own = dot(hs, back[:, :256], ((0,), (0,)))
    code_rest, d_out, wus_far, wds_far = barrier((code_rest, d_out, wus_far, wds_far))
    code_own, code_other = in_order(code_half, code_rest)
    code = jnp.concatenate([code_own, code_other], 0)
    u_out = bf(dot(code[:, 256:], cs, ((0,), (0,))))
    u_in = send(u_out, rep_pair(0))
    u_out, code_other = barrier((u_out, code_other))
    code_far = send(code_other, rep_pair(1))
    code_own, code, u_out, back_far = barrier((code_own, code, u_out, back_far))
    r_own = dot(code_own, wus, ((1,), (0,)))
    u_own = dot(code[:, :256], cs, ((0,), (0,)))
    r_own, u_own = barrier((r_own, u_own))
    grad_hidden = bf(g_own + dot(back_far, wds_far, ((1,), (1,))))
    grad_down = bf(d_own + f32(d_in))
    rebuilt = bf(r_own + dot(code_far, wus_far, ((1,), (0,))))
    grad_hidden, grad_down, rebuilt, u_in = barrier((grad_hidden, grad_down, rebuilt, u_in))
    grad_up = bf(u_own + f32(u_in))
    return (rebuilt[None], grad_hidden[None], grad_up[None], grad_down[None])


def solution(mesh):
    return jax.shard_map(
        shards,
        mesh=mesh,
        in_specs=(
            P("section", "rep", "tp"),
            P("section", "rep", "tp"),
            P("section", "tp", "rep"),
            P("section", "rep", "tp"),
        ),
        out_specs=(
            P("section", "rep", "tp"),
            P("section", "rep", "tp"),
            P("section", "rep", "tp"),
            P("section", "tp", "rep"),
        ),
        check_vma=False,
    )
```
